256 devices in a mesh: dp: 16 (over z, y_hi), fsdp: 16 (over y_lo, x, core).
Axes of the slice: x: 4, y: 4 (y_hi: 2, y_lo: 2; y = y_hi * 2 + y_lo), z: 8, core: 2. Of those that a mesh axis runs over, the one named last changes fastest.
Arguments:
- activations: bfloat16 [131072, 4096], P(('dp', 'fsdp')), may hold values from -6 to 6
- cotangent: bfloat16 [131072, 4096], P(('dp', 'fsdp')), may hold values from -0.0625 to 0.0625
- basis: bfloat16 [4096, 1024], P('fsdp'), may hold values from -0.09375 to 0.09375
- weight: bfloat16 [4096, 4096], P(None, 'fsdp'), may hold values from -6 to 6
- first: float32 [1024, 16, 16, 16], P(None, 'fsdp', 'dp'), may hold values from -6 to 6
- second: float32 [1024, 16, 16, 16], P(None, 'fsdp', 'dp'), may hold values from 0.25 to 4
Outputs:
- new_weight: bfloat16 [4096, 4096], P(None, 'fsdp')
- new_first: float32 [1024, 16, 16, 16], P(None, 'fsdp', 'dp')
- new_second: float32 [1024, 16, 16, 16], P(None, 'fsdp', 'dp')
The draws below stay inside these ranges and needn't reach their ends.
All inputs are finite; a program needn't handle non-finite values.
Results may differ from the reference program's by a relative error of at most 0.0045.
Values may be sent and summed in bfloat16 or wider, within the bound.
No kernel may reach another device: no remote copies, remote signals or barrier semaphores. Data moves between devices by JAX's collectives and lax.ppermute only.
A program may use at most 128 MiB of HBM per device.

```python
import math
import jax
import jax.numpy as jnp

D = 4096
RANK = 1024
TOKENS = 131072
OWN = 16
N_DP = 16
N_FSDP = 16


def with_spikes(drawn, stream_key, source, target, parts, factor):
    def block_of(position):
        return (jnp.arange(drawn.shape[position]) // (drawn.shape[position] // parts)).reshape((-1,) + (1,) * (drawn.ndim - 1 - position))

    near = jax.random.permutation(stream_key, parts)[block_of(target)]
    second = (block_of(target) + parts // 2) % parts
    return jnp.where((block_of(source) == near) | (block_of(source) == second), factor * drawn, drawn)


def shard_levels(rng, shape, cuts, smallest, top_value):
    def one(dim, parts):
        draws = jax.random.uniform(jax.random.fold_in(jax.random.fold_in(rng, 6), dim), (parts,), jnp.float32, smallest / len(cuts), top_value / len(cuts))
        return jnp.repeat(jnp.exp(draws), shape[dim] // parts).reshape((-1,) + (1,) * (len(shape) - dim - 1))

    loudness = one(*cuts[0])
    for cut in cuts[1:]:
        loudness = loudness * one(*cut)
    return loudness


def centred(key, extent, spread, bound, split=(), dtype=jnp.bfloat16):
    array = jax.random.normal(key, extent, jnp.float32) * spread
    if len(split) > 0:
        array = shard_levels(key, extent, split, -0.22, 0.18) * array
    return jnp.clip(array, min=-bound, max=bound).astype(dtype)


def bell_draw_with(own_key, shape, scale, reach, pieces, heavy, kind=jnp.bfloat16):
    result = scale * jax.random.normal(own_key, shape, jnp.float32)
    if pieces:
        result = result * shard_levels(own_key, shape, pieces, -0.22, 0.18)
    return jnp.clip(with_spikes(result, jax.random.fold_in(own_key, 3), *heavy), -reach, reach).astype(kind)


def setup_inputs(seed: int = 0) -> dict:
    splits = jax.random.split(jax.random.key(seed), 7)
    return {
        "activations": centred(splits[0], (TOKENS, D), 1.0, 6.0, ((0, 256),)),
        "cotangent": bell_draw_with(splits[1], (TOKENS, D), (TOKENS ** -0.5), 0.0625, ((0, 256),), (0, 1, 256, 6.0)),
        "basis": centred(splits[2], (D, RANK), D ** -0.5, 0.09375, ((0, 16),)),
        "weight": centred(splits[3], (D, D), 1.0, 6.0, ((1, 16),)),
        "first": centred(splits[4], (RANK, N_FSDP, N_DP, OWN), 1.0, 6.0, ((1, 16), (2, 16)), jnp.float32),
        "second": jnp.clip(jnp.exp(math.log(4.0) - 2.7725887 * jax.random.uniform(splits[5], (RANK, N_FSDP, N_DP, OWN), jnp.float32) ** shard_levels(splits[5], (RANK, N_FSDP, N_DP, OWN), ((1, 16), (2, 16)), -0.2, 0.2)), 0.25, 4.0),
    }


beta_one = 0.9
beta_two = 0.999
corr_one = 1.0 - math.exp(1000.0 * math.log(0.9))
corr_two = 1.0 - math.exp(1000.0 * math.log(0.999))
epsilon = 1e-08
rate = 0.5

def reference(activations, cotangent, basis, weight, first, second):
    projected = jnp.dot(activations, basis, preferred_element_type=jnp.float32).astype(jnp.bfloat16)
    gradient = jnp.dot(projected.T, cotangent, preferred_element_type=jnp.float32)
    gradient = gradient.reshape(RANK, N_FSDP, N_DP, OWN)
    moment_one = beta_one * first + (1.0 - beta_one) * gradient
    moment_two = beta_two * second + (1.0 - beta_two) * gradient * gradient
    update = moment_one / corr_one / (jnp.sqrt(moment_two / corr_two) + epsilon)
    update = update.astype(jnp.bfloat16).reshape(RANK, D)
    expanded = jnp.dot(basis, update, preferred_element_type=jnp.float32)
    new_weight = (weight.astype(jnp.float32) - rate * expanded).astype(jnp.bfloat16)
    return (new_weight, moment_one, moment_two)
```

```python
import math

import jax
import jax.numpy as jnp
from jax import lax
from jax.sharding import PartitionSpec as P

beta_one = 0.9
beta_two = 0.999
corr_one = 1.0 - math.exp(1000.0 * math.log(0.9))
corr_two = 1.0 - math.exp(1000.0 * math.log(0.999))
epsilon = 1e-08
rate = 0.5


def body(activations, cotangent, basis, weight, first, second):
    low_rank = basis.shape[1]
    owned = first.shape[-1]
    rows = lax.all_gather(basis, "fsdp", axis=0, tiled=True)
    projected = jnp.dot(activations, rows, preferred_element_type=jnp.float32)
    projected = projected.astype(jnp.bfloat16)
    gradient = lax.dot_general(
        cotangent, projected, (((0,), (0,)), ((), ())), preferred_element_type=jnp.float32
    )
    partial_sum = lax.psum_scatter(
        gradient.astype(jnp.bfloat16), "fsdp", scatter_dimension=0, tiled=True
    )
    summed = lax.psum_scatter(partial_sum, "dp", scatter_dimension=0, tiled=True)
    summed = summed.astype(jnp.float32)
    moment_one = beta_one * first.reshape(low_rank, owned).T + (1.0 - beta_one) * summed
    moment_two = beta_two * second.reshape(low_rank, owned).T + (1.0 - beta_two) * summed * summed
    update = moment_one / corr_one / (jnp.sqrt(moment_two / corr_two) + epsilon)
    update = lax.all_gather(update.astype(jnp.bfloat16), "dp", axis=0, tiled=True)
    expanded = lax.dot_general(
        rows, update, (((1,), (1,)), ((), ())), preferred_element_type=jnp.float32
    )
    new_weight = (weight.astype(jnp.float32) - rate * expanded).astype(jnp.bfloat16)
    return (new_weight, moment_one.T.reshape(first.shape), moment_two.T.reshape(first.shape))


def solution(mesh):
    in_specs = (
        P(("dp", "fsdp"), None),
        P(("dp", "fsdp"), None),
        P("fsdp", None),
        P(None, "fsdp"),
        P(None, "fsdp", "dp", None),
        P(None, "fsdp", "dp", None),
    )
    out_specs = (P(None, "fsdp"), P(None, "fsdp", "dp", None), P(None, "fsdp", "dp", None))
    return jax.shard_map(body, mesh=mesh, in_specs=in_specs, out_specs=out_specs, check_vma=False)
```

```python
import math

import jax
import jax.numpy as jnp
from jax import lax
from jax.experimental import pallas as pl
from jax.experimental.pallas import tpu as pltpu
from jax.sharding import PartitionSpec as P

beta_one = 0.9
beta_two = 0.999
corr_one = 1.0 - math.exp(1000.0 * math.log(0.9))
corr_two = 1.0 - math.exp(1000.0 * math.log(0.999))
epsilon = 1e-08
rate = 0.5

AXES = ("dp", "fsdp")
NX, NY, NZ = 4, 4, 8
RING_Y = (0, 2, 1, 3)
VMEM = 56 * 2**20


def place(x, y, z, c):
    return (z * 2 + y // 2) * 16 + ((y % 2) * 4 + x) * 2 + c


CHIPS = [(x, y, z) for z in range(NZ) for y in range(NY) for x in range(NX)]


def shift(value, dx=0, dy=0, swap=False):
    pairs = [
        (place(x, y, z, c), place((x + dx) % NX, (y + dy) % NY, z, 1 - c if swap else c))
        for x, y, z in CHIPS
        for c in range(2)
    ]
    return lax.ppermute(value, AXES, sorted(pairs))


def along_x(c):
    return [[place(x, y, z, c) for x in range(NX)] for z in range(NZ) for y in range(NY)]


def along_y(c):
    return [[place(x, y, z, c) for y in RING_Y] for z in range(NZ) for x in range(NX)]


def along_zc():
    return [
        [place(x, y, z, c) for z in range(NZ) for c in range(2)]
        for y in range(NY)
        for x in range(NX)
    ]


def exchange(value, groups):
    return lax.all_to_all(value, AXES, 0, 0, tiled=True, axis_index_groups=groups)


def dot(a, b, dims):
    return lax.dot_general(a, b, (dims, ((), ())), preferred_element_type=jnp.float32)


def project_kernel(layout, first, order, own, other, *refs):
    count = sum(layout)
    pieces, rest = refs[:count], refs[count:]
    if first:
        total, stacked = rest
        result = None
    else:
        before, result, stacked, total = rest
    step = pl.program_id(0)
    half = own.shape[0]

    @pl.when(step == 0)
    def _():
        total[...] = jnp.zeros_like(total) if first else before[...]

    at = 0
    for j, n in enumerate(layout):
        mine = pieces[at : at + n]
        at += n

        @pl.when(step == j)
        def _(mine=mine):
            done = 0
            for piece in mine:
                rows = piece.shape[0]
                stacked[0, done : done + rows, :] = piece[...]
                for i, block in enumerate((own, other)):
                    total[i * half : (i + 1) * half, :] += dot(
                        block[:, done : done + rows], piece[...], ((1,), (0,))
                    )
                done += rows

    if not first:

        @pl.when(step == len(layout) - 1)
        def _():
            result[...] = total[...].astype(result.dtype)


def project(order, own, other, groups, before=None):
    layout = [len(g) for g in groups]
    pieces = [p for g in groups for p in g]
    n, (half, _) = len(groups), own.shape
    depth, low = sum(p.shape[0] for p in groups[0]), pieces[0].shape[1]
    whole = lambda a: pl.BlockSpec(a.shape, lambda j, o: (0,) * a.ndim)
    block = pl.BlockSpec((half, depth), lambda j, o: (0, o[j]))
    stacked = jax.ShapeDtypeStruct((n, depth, low), jnp.bfloat16)
    stack_spec = pl.BlockSpec((1, depth, low), lambda j, o: (j, 0, 0))
    total = jax.ShapeDtypeStruct((2 * half, low), jnp.float32)
    ins = [block, block] + [whole(p) for p in pieces]
    args = [own, other] + pieces
    scratch = []
    if before is None:
        outs, out_specs = [total, stacked], [whole(total), stack_spec]
    else:
        ins.append(whole(before))
        args.append(before)
        result = jax.ShapeDtypeStruct(total.shape, jnp.bfloat16)
        outs, out_specs = [result, stacked], [whole(result), stack_spec]
        scratch = [pltpu.VMEM(total.shape, jnp.float32)]

    def kernel(*refs):
        project_kernel(layout, before is None, *refs)

    return pl.pallas_call(
        kernel,
        grid_spec=pltpu.PrefetchScalarGridSpec(
            num_scalar_prefetch=1,
            grid=(n,),
            in_specs=ins,
            out_specs=out_specs,
            scratch_shapes=scratch,
        ),
        out_shape=outs,
        cost_estimate=pl.CostEstimate(
            flops=4 * half * depth * n * low, bytes_accessed=16 * 2**20, transcendentals=0
        ),
        compiler_params=pltpu.CompilerParams(vmem_limit_bytes=VMEM),
    )(order, *args)


def gradient_kernel(core, own, other, projected, out, tile):
    half = own.shape[0]
    high = pl.program_id(1)

    @pl.when(high == 0)
    def _():
        total = dot(own[...], projected[:half, :], ((0,), (0,)))
        total += dot(other[...], projected[half:, :], ((0,), (0,)))
        tile[...] = total.astype(tile.dtype)

    for h in range(2):

        @pl.when(high == h)
        def _(h=h):
            for z in range(NZ):
                for c in range(2):
                    at = c * 256 + z * 32 + h * 16
                    to = z * 32 + c * 16
                    out[0, 0, to : to + 16, :] = tile[at : at + 16, :]


def gradient(core, own, other, projected):
    half, width = own.shape
    low = projected.shape[1]
    cols = width // 8

    def place_out(t, h, c):
        x, y = t % 4, (t // 4) * 2 + h
        return jnp.where(c[0] == 0, x, y), jnp.where(c[0] == 0, y, x), 0, 0

    block = pl.BlockSpec((half, cols), lambda t, h, c: (0, t))
    return pl.pallas_call(
        gradient_kernel,
        grid_spec=pltpu.PrefetchScalarGridSpec(
            num_scalar_prefetch=1,
            grid=(8, 2),
            in_specs=[
                block,
                block,
                pl.BlockSpec(projected.shape, lambda t, h, c: (0, 0)),
            ],
            out_specs=pl.BlockSpec((1, 1, cols // 2, low), place_out),
            scratch_shapes=[pltpu.VMEM((cols, low), jnp.bfloat16)],
        ),
        out_shape=jax.ShapeDtypeStruct((4, 4, cols // 2, low), jnp.bfloat16),
        cost_estimate=pl.CostEstimate(
            flops=4 * half * width * low, bytes_accessed=14 * 2**20, transcendentals=0
        ),
        compiler_params=pltpu.CompilerParams(vmem_limit_bytes=VMEM),
    )(core, own, other, projected)


def expand_kernel(order, core, mine_a, mine_b, rest_a, rest_b, near, far, weight, out):
    step = pl.program_id(0)

    def write(mine, rest):
        total = dot(mine[0], near[...], ((1,), (1,)))
        total += dot(rest[0], far[...], ((1,), (1,)))
        out[...] = (weight[...].astype(jnp.float32) - rate * total).astype(out.dtype)

    @pl.when(step < 4)
    def _():
        write(mine_a, rest_a)

    @pl.when(step >= 4)
    def _():
        write(mine_b, rest_b)


def expand(order, core, mine, rest, update, weight):
    _, depth, low = mine[0].shape
    cols = weight.shape[1]
    early = pl.BlockSpec((1, depth, low), lambda j, o, c: (jnp.minimum(j, 3), 0, 0))
    late = pl.BlockSpec((1, depth, low), lambda j, o, c: (jnp.maximum(j - 4, 0), 0, 0))
    rows = pl.BlockSpec((depth, cols), lambda j, o, c: (o[j], 0))
    return pl.pallas_call(
        expand_kernel,
        grid_spec=pltpu.PrefetchScalarGridSpec(
            num_scalar_prefetch=2,
            grid=(8,),
            in_specs=[
                early,
                late,
                early,
                late,
                pl.BlockSpec((cols, low), lambda j, o, c: (0, c[0])),
                pl.BlockSpec((cols, low), lambda j, o, c: (0, 1 - c[0])),
                rows,
            ],
            out_specs=rows,
        ),
        out_shape=jax.ShapeDtypeStruct(weight.shape, weight.dtype),
        cost_estimate=pl.CostEstimate(
            flops=4 * weight.size * low, bytes_accessed=13 * 2**20, transcendentals=0
        ),
        compiler_params=pltpu.CompilerParams(vmem_limit_bytes=VMEM),
    )(order, core, *mine, *rest, update, update, weight)


def added(value):
    return jnp.sum(value.astype(jnp.float32), axis=0).astype(jnp.bfloat16)


def body(activations, cotangent, basis, weight, first, second):
    low_rank = basis.shape[1]
    half = low_rank // 2
    owned = first.shape[-1]
    f = lax.axis_index("fsdp")
    core, x, y_lo = f % 2, (f // 2) % 4, f // 8
    order = jnp.stack(
        [
            side * 4 + (x + step) % 4
            for side, step in (
                (y_lo, 0),
                (y_lo, 3),
                (y_lo, 1),
                (1 - y_lo, 0),
                (y_lo, 2),
                (1 - y_lo, 3),
                (1 - y_lo, 1),
                (1 - y_lo, 2),
            )
        ]
    ).astype(jnp.int32)
    core_id = core.reshape(1).astype(jnp.int32)

    left, right = basis[:, :half], basis[:, half:]
    kept = jnp.where(core == 0, left, right)
    came = shift(jnp.where(core == 0, right, left), swap=True)
    top = jnp.where(core == 0, kept, came)
    bottom = jnp.where(core == 0, came, kept)
    chip = jnp.concatenate([top, bottom], axis=0)
    other_activations = shift(activations, swap=True)
    other_cotangent = shift(cotangent, swap=True)

    back = shift(chip, dx=1)
    ahead = shift(chip, dx=-1)
    across_top = shift(top, dy=1)
    across_bottom = shift(bottom, dy=-1)
    rows = top.shape[0]
    far_top = shift(back[:rows], dx=1)
    far_bottom = shift(ahead[rows:], dx=-1)
    across_back = shift(back, dy=1)
    across_ahead = shift(ahead, dy=-1)
    across_far_top = shift(far_top, dy=1)
    across_far_bottom = shift(far_bottom, dy=-1)

    begun, stacked_a = project(
        order[:4],
        activations,
        other_activations,
        [(chip,), (back,), (ahead,), (across_top, across_bottom)],
    )
    projected, stacked_b = project(
        order[4:],
        activations,
        other_activations,
        [
            (far_top, far_bottom),
            (across_back,),
            (across_ahead,),
            (across_far_top, across_far_bottom),
        ],
        begun,
    )
    rest = (shift(stacked_a, swap=True), shift(stacked_b, swap=True))

    terms = gradient(core_id, cotangent, other_cotangent, projected)
    terms = added(exchange(terms, along_x(0) + along_y(1)))
    terms = added(exchange(terms, along_y(0) + along_x(1)))
    terms = exchange(terms.reshape(16, owned, half), along_zc())
    summed = jnp.sum(terms.reshape(NZ, 2, owned, half).astype(jnp.float32), axis=0)
    summed = summed.transpose(1, 0, 2).reshape(owned, low_rank)

    moment_one = beta_one * first.reshape(low_rank, owned).T + (1.0 - beta_one) * summed
    moment_two = beta_two * second.reshape(low_rank, owned).T + (1.0 - beta_two) * summed * summed
    update = moment_one / corr_one / (jnp.sqrt(moment_two / corr_two) + epsilon)
    update = update.astype(jnp.bfloat16)
    copies = jnp.broadcast_to(update[None], (16, owned, low_rank))
    update = lax.all_to_all(copies, "dp", 0, 0, tiled=True).reshape(16 * owned, low_rank)

    new_weight = expand(order, core_id, (stacked_a, stacked_b), rest, update, weight)
    return (new_weight, moment_one.T.reshape(first.shape), moment_two.T.reshape(first.shape))


def solution(mesh):
    in_specs = (
        P(("dp", "fsdp"), None),
        P(("dp", "fsdp"), None),
        P("fsdp", None),
        P(None, "fsdp"),
        P(None, "fsdp", "dp", None),
        P(None, "fsdp", "dp", None),
    )
    out_specs = (P(None, "fsdp"), P(None, "fsdp", "dp", None), P(None, "fsdp", "dp", None))
    return jax.shard_map(body, mesh=mesh, in_specs=in_specs, out_specs=out_specs, check_vma=False)
```

```python
import math

import jax
import jax.numpy as jnp
import numpy as np
from jax import lax
from jax.experimental import pallas as pl
from jax.experimental.pallas import tpu as pltpu
from jax.sharding import PartitionSpec as P

beta_one = 0.9
beta_two = 0.999
corr_one = 1.0 - math.exp(1000.0 * math.log(0.9))
corr_two = 1.0 - math.exp(1000.0 * math.log(0.999))
epsilon = 1e-08
rate = 0.5

AXES = ("dp", "fsdp")
NX, NY, NZ = 4, 4, 8
VMEM = 56 * 2**20


def place(x, y, z, c):
    return (z * 2 + y // 2) * 16 + ((y % 2) * 4 + x) * 2 + c


CHIPS = [(x, y, z) for z in range(NZ) for y in range(NY) for x in range(NX)]


def route(value, where):
    pairs = []
    for x, y, z in CHIPS:
        for c in range(2):
            tx, ty, tz, tc = where(x, y, z, c)
            pairs.append((place(x, y, z, c), place(tx % NX, ty % NY, tz % NZ, tc)))
    return lax.ppermute(value, AXES, sorted(pairs))


def swap(value):
    return route(value, lambda x, y, z, c: (x, y, z, 1 - c))


def ring_x(value):
    return route(value, lambda x, y, z, c: (x + 1 - 2 * c, y, z, c))


def ring_y(value):
    return route(value, lambda x, y, z, c: (x, y + 1 - 2 * c, z, c))


def along(value, by, first):
    return route(
        value,
        lambda x, y, z, c: (x + by, y, z, c) if (c == 0) == first else (x, y + by, z, c),
    )


def together(*values):
    return lax.optimization_barrier(values)


def along_zc():
    return [
        [place(x, y, z, c) for z in range(NZ) for c in range(2)]
        for y in range(NY)
        for x in range(NX)
    ]


def exchange(value, groups):
    return lax.all_to_all(value, AXES, 0, 0, tiled=True, axis_index_groups=groups)


def dot(a, b, dims):
    return lax.dot_general(a, b, (dims, ((), ())), preferred_element_type=jnp.float32)


HBM = pl.BlockSpec(memory_space=pltpu.HBM)


def run(kernel, table, args, outs, scratch, copies, flops, moved):
    return pl.pallas_call(
        kernel,
        grid_spec=pltpu.PrefetchScalarGridSpec(
            num_scalar_prefetch=1,
            grid=(),
            in_specs=[HBM] * len(args),
            out_specs=[HBM] * len(outs),
            scratch_shapes=[pltpu.VMEM(shape, dtype) for shape, dtype in scratch]
            + [pltpu.SemaphoreType.DMA((copies,))],
        ),
        out_shape=outs,
        cost_estimate=pl.CostEstimate(flops=flops, bytes_accessed=moved, transcendentals=0),
        compiler_params=pltpu.CompilerParams(vmem_limit_bytes=VMEM),
    )(table, *args)


class Copies:
    def __init__(self, sems):
        self.sems, self.used = sems, 0

    def __call__(self, source, target):
        copy = pltpu.make_async_copy(source, target, self.sems.at[self.used])
        self.used += 1
        copy.start()
        return copy


def fetch_pieces(copies, table, phase, own, other, pieces, blocks, basis):
    half, (depth, low_rank) = own.shape[0], pieces[0].shape
    low, started = low_rank // 2, []
    lanes = pl.ds(pl.multiple_of(table[CORE] * low, low), low)
    for j, piece in enumerate(pieces):
        at = pl.ds(j * depth, depth)
        columns = pl.ds(pl.multiple_of(table[PIECES[phase] + j] * depth, depth), depth)
        started += [
            copies(own.at[:, columns], blocks.at[:half, at]),
            copies(other.at[:, columns], blocks.at[half:, at]),
            copies(piece.at[:, lanes], basis.at[at, :]),
        ]
    return started


def wait(copies):
    for copy in copies:
        copy.wait()


def project(table, phase, own, other, pieces, before=None):
    n, half = len(pieces), own.shape[0]
    depth, low = pieces[0].shape[0], pieces[0].shape[1] // 2
    total = jax.ShapeDtypeStruct((2 * half, low), jnp.float32)
    extra = [] if before is None else [before]

    def kernel(table, own, other, *refs):
        pieces, (out, blocks, basis, total, sems) = refs[:n], refs[-5:]
        copies = Copies(sems)
        started = fetch_pieces(copies, table, phase, own, other, pieces, blocks, basis)
        if extra:
            started.append(copies(refs[n], total))
        wait(started)
        ended = []
        for m in range(4):
            rows = pl.ds(m * half // 2, half // 2)
            part = dot(blocks[rows, :], basis[...], ((1,), (0,)))
            total[rows, :] = total[rows, :] + part if extra else part
            ended.append(copies(total.at[rows, :], out.at[rows, :]))
        wait(ended)

    return run(
        kernel,
        table,
        (own, other, *pieces, *extra),
        [total],
        [
            ((2 * half, n * depth), jnp.bfloat16),
            ((n * depth, low), jnp.bfloat16),
            (total.shape, jnp.float32),
        ],
        3 * n + 5,
        4 * half * depth * n * low,
        n * 2**20,
    )[0]


def fetch_tiles(copies, table, call, near, far, tiles):
    half, cols = near.shape[0], tiles.shape[2]
    started = []
    for j in range(4):
        at = table[TILES[call] + 5 * j]
        columns = pl.ds(pl.multiple_of(at * cols, cols), cols)
        started.append(
            [
                copies(near.at[:, columns], tiles.at[j, :half]),
                copies(far.at[:, columns], tiles.at[j, half:]),
            ]
        )
    return started


def write_tiles(sems, table, call, started, tiles, projected, dealt, outs):
    def each_out(j, h, act):
        at = TILES[call] + 5 * j + 1 + 2 * h
        for w, out in enumerate(outs):

            @pl.when(table[at] == w)
            def _(out=out):
                target = out.at[table[at + 1]]
                act(pltpu.make_async_copy(dealt.at[j, h], target, sems.at[2 * j + h]))

    for j in range(4):
        wait(started[j])
        total = dot(tiles[j], projected[...], ((0,), (0,))).astype(jnp.bfloat16)
        for h in range(2):
            for z in range(NZ):
                for c in range(2):
                    row = c * 256 + z * 32 + h * 16
                    to = z * 32 + c * 16
                    dealt[j, h, to : to + 16, :] = total[row : row + 16, :]
            each_out(j, h, lambda copy: copy.start())
    for j in range(4):
        for h in range(2):
            each_out(j, h, lambda copy: copy.wait())


def gradient_shapes(near, low):
    half, width = near.shape
    cols = width // 8
    slots = jax.ShapeDtypeStruct((4, cols // 2, low), jnp.bfloat16)
    scratch = [
        ((4, 2 * half, cols), jnp.bfloat16),
        ((2 * half, low), jnp.bfloat16),
        ((4, 2, cols // 2, low), jnp.bfloat16),
    ]
    return slots, scratch


def finish(table, own, other, pieces, before, near, far):
    half, width = own.shape
    n, depth, low = len(pieces), pieces[0].shape[0], pieces[0].shape[1] // 2
    slots, scratch = gradient_shapes(near, low)

    def kernel(table, own, other, *refs):
        pieces, (before, near, far, out, first, second) = refs[:n], refs[n : n + 6]
        blocks, basis, total, tiles, projected, dealt, sems = refs[n + 6 :]
        copies = Copies(sems.at[pl.ds(8, 3 * n + 10)])
        started = fetch_pieces(copies, table, 2, own, other, pieces, blocks, basis)
        started.append(copies(before, total))
        fetched = fetch_tiles(copies, table, 0, near, far, tiles)
        wait(started)
        for m in range(4):
            rows = pl.ds(m * half // 2, half // 2)
            part = dot(blocks[rows, :], basis[...], ((1,), (0,)))
            projected[rows, :] = (total[rows, :] + part).astype(projected.dtype)
        kept = copies(projected, out)
        write_tiles(sems, table, 0, fetched, tiles, projected, dealt, (first, second))
        kept.wait()

    return run(
        kernel,
        table,
        (own, other, *pieces, before, near, far),
        [jax.ShapeDtypeStruct((2 * half, low), jnp.bfloat16), slots, slots],
        [
            ((2 * half, n * depth), jnp.bfloat16),
            ((n * depth, low), jnp.bfloat16),
            (before.shape, jnp.float32),
            *scratch,
        ],
        3 * n + 18,
        2 * half * width * low,
        11 * 2**20,
    )


def gradient(table, near, far, projected):
    half, width = near.shape
    low = projected.shape[1]
    slots, scratch = gradient_shapes(near, low)

    def kernel(table, near, far, source, first, second, tiles, projected, dealt, sems):
        copies = Copies(sems.at[pl.ds(8, 9)])
        started = copies(source, projected)
        fetched = fetch_tiles(copies, table, 1, near, far, tiles)
        started.wait()
        write_tiles(sems, table, 1, fetched, tiles, projected, dealt, (first, second))

    return run(
        kernel,
        table,
        (near, far, projected),
        [slots, slots],
        scratch,
        17,
        2 * half * width * low,
        7 * 2**20,
    )


def expand(table, mine, rest, update, weight):
    depth, low_rank = mine[0].shape
    cols = weight.shape[1]
    n = len(mine)

    def kernel(table, *refs):
        update, weight, out, held, factor, old, new, sems = refs[2 * n :]
        copies = Copies(sems)
        first = copies(update, factor)
        started = []
        for j in range(n):
            for i, side in ((j, table[CORE]), (n + j, 1 - table[CORE])):
                at = pl.multiple_of((2 * table[SHARDS + j] + side) * depth, depth)
                rows = pl.ds(at, depth)
                loads = [copies(refs[i], held.at[i]), copies(weight.at[rows, :], old.at[i])]
                started.append((i, rows, loads))
        first.wait()
        ended = []
        for i, rows, loads in started:
            wait(loads)
            total = dot(held[i], factor[...], ((1,), (1,)))
            new[i] = (old[i].astype(jnp.float32) - rate * total).astype(new.dtype)
            ended.append(copies(new.at[i], out.at[rows, :]))
        wait(ended)

    return run(
        kernel,
        table,
        (*mine, *rest, update, weight),
        [jax.ShapeDtypeStruct(weight.shape, weight.dtype)],
        [
            ((2 * n, depth, low_rank), jnp.bfloat16),
            (update.shape, jnp.bfloat16),
            ((2 * n, depth, cols), jnp.bfloat16),
            ((2 * n, depth, cols), jnp.bfloat16),
        ],
        6 * n + 1,
        2 * weight.size * low_rank,
        13 * 2**20,
    )[0]


def added(*values):
    return sum(v.astype(jnp.float32) for v in values).astype(jnp.bfloat16)


def tile_rows(core, x, y, call):
    low, rows = y % 2, []
    for j in range(4):
        if core == 0:
            rows.append((j % 2) * 4 + (x + ((2, 0), (1, 3))[call][j // 2]) % 4)
            for h in range(2):
                rows += [j // 2, (h * 2 + j % 2 - y) % 4]
        else:
            side = low if call == 0 else 1 - low
            rows.append(side * 4 + (x + j) % 4)
            for h in range(2):
                rows += [int((h * 2 + side - y) % 4 != 2 - call), j]
    return rows


TURNED = [4 * (j // 4) + (4 - j) % 4 for j in range(8)]
PHASES = ((0, 1, 4), (2, 5, 3, 6), (7,))
CORE, SHARDS, TILES, PIECES = 0, 1, (9, 29), (49, 55, 63)


def device_row(y_hi, y_lo, x, core):
    shards = [((y_lo + j // 4) % 2) * 4 + (x + (2 * core - 1) * j) % 4 for j in range(8)]
    row = [core] + shards
    for call in range(2):
        row += tile_rows(core, x, 2 * y_hi + y_lo, call)
    for phase in PHASES:
        for j in phase:
            row += [2 * shards[j] + core, 2 * shards[TURNED[j]] + 1 - core]
    return row


def device_table():
    rows = [
        device_row(y_hi, y_lo, x, core)
        for y_hi in range(2)
        for y_lo in range(2)
        for x in range(4)
        for core in range(2)
    ]
    return np.array(rows, np.int32)


def body(activations, cotangent, basis, weight, first, second):
    low_rank = basis.shape[1]
    half = low_rank // 2
    owned = first.shape[-1]
    f, d = lax.axis_index("fsdp"), lax.axis_index("dp")
    table = lax.dynamic_index_in_dim(device_table(), (d % 2) * 16 + f, 0, keepdims=False)

    x1, y0, s_x0, other_activations, cotangent = together(
        ring_x(basis), ring_y(basis), swap(basis), swap(activations), cotangent
    )
    x2, y1, s_x1, s_y0, other_cotangent, x1, y0 = together(
        ring_x(x1), ring_y(x1), swap(x1), swap(y0), swap(cotangent), x1, y0
    )
    both = (activations, other_activations)
    begun = project(table, 0, *both, [basis, s_x0, x1, s_x1, y0, s_y0])
    x3, y2, s_x2, s_y1, begun, x2, y1 = together(
        ring_x(x2), ring_y(x2), swap(x2), swap(y1), begun, x2, y1
    )
    s_x3, s_y2 = swap(x3), swap(y2)
    begun = project(table, 1, *both, [x2, s_x2, y1, s_y1, x3, s_x3, y2, s_y2], begun)
    y3, begun = together(ring_y(x3), begun)
    s_y3 = swap(y3)
    projected, opposite, own = finish(
        table, *both, (y3, s_y3), begun, cotangent, other_cotangent
    )
    mine = (basis, x1, x2, x3, y0, y1, y2, y3)
    rest = (s_x0, s_x1, s_x2, s_x3, s_y0, s_y1, s_y2, s_y3)
    rest = tuple(rest[j] for j in TURNED)

    came = along(opposite, 2, True)
    following, previous = gradient(table, cotangent, other_cotangent, projected)
    (own,) = together(added(own, came))
    terms = (own, along(following, 1, True), along(previous, -1, True))
    own, following, opposite, previous = [added(*(t[i] for t in terms)) for i in range(4)]
    terms = added(
        own,
        along(opposite, 2, False),
        along(following, 1, False),
        along(previous, -1, False),
    )
    terms = exchange(terms.reshape(16, owned, half), along_zc())
    summed = jnp.sum(terms.reshape(NZ, 2, owned, half).astype(jnp.float32), axis=0)
    summed = summed.transpose(1, 0, 2).reshape(owned, low_rank)

    moment_one = beta_one * first.reshape(low_rank, owned).T + (1.0 - beta_one) * summed
    moment_two = beta_two * second.reshape(low_rank, owned).T + (1.0 - beta_two) * summed * summed
    update = moment_one / corr_one / (jnp.sqrt(moment_two / corr_two) + epsilon)
    update = update.astype(jnp.bfloat16)
    copies = jnp.broadcast_to(update[None], (16, owned, low_rank))
    update = lax.all_to_all(copies, "dp", 0, 0, tiled=True).reshape(16 * owned, low_rank)

    new_weight = expand(table, mine, rest, update, weight)
    return (new_weight, moment_one.T.reshape(first.shape), moment_two.T.reshape(first.shape))


def solution(mesh):
    in_specs = (
        P(("dp", "fsdp"), None),
        P(("dp", "fsdp"), None),
        P("fsdp", None),
        P(None, "fsdp"),
        P(None, "fsdp", "dp", None),
        P(None, "fsdp", "dp", None),
    )
    out_specs = (P(None, "fsdp"), P(None, "fsdp", "dp", None), P(None, "fsdp", "dp", None))
    return jax.shard_map(body, mesh=mesh, in_specs=in_specs, out_specs=out_specs, check_vma=False)
```

```python
import math

import jax
import jax.numpy as jnp
import numpy as np
from jax import lax
from jax.experimental import pallas as pl
from jax.experimental.pallas import tpu as pltpu
from jax.sharding import PartitionSpec as P

beta_one = 0.9
beta_two = 0.999
corr_one = 1.0 - math.exp(1000.0 * math.log(0.9))
corr_two = 1.0 - math.exp(1000.0 * math.log(0.999))
epsilon = 1e-08
rate = 0.5

AXES = ("dp", "fsdp")
NX, NY, NZ = 4, 4, 8
SMALL, LARGE = 16 * 2**20, 56 * 2**20


def place(x, y, z, c):
    return (z * 2 + y // 2) * 16 + ((y % 2) * 4 + x) * 2 + c


CHIPS = [(x, y, z) for z in range(NZ) for y in range(NY) for x in range(NX)]


def route(value, where):
    pairs = []
    for x, y, z in CHIPS:
        for c in range(2):
            tx, ty, tz, tc = where(x, y, z, c)
            pairs.append((place(x, y, z, c), place(tx % NX, ty % NY, tz % NZ, tc)))
    return lax.ppermute(value, AXES, sorted(pairs))


def swap(value):
    return route(value, lambda x, y, z, c: (x, y, z, 1 - c))


def ring_x(value):
    return route(value, lambda x, y, z, c: (x + 1 - 2 * c, y, z, c))


def ring_y(value):
    return route(value, lambda x, y, z, c: (x, y + 1 - 2 * c, z, c))


def along(value, by, first):
    return route(
        value,
        lambda x, y, z, c: (x + by, y, z, c) if (c == 0) == first else (x, y + by, z, c),
    )


def together(*values):
    return lax.optimization_barrier(values)


def along_zc():
    return [
        [place(x, y, z, c) for z in range(NZ) for c in range(2)]
        for y in range(NY)
        for x in range(NX)
    ]


def exchange(value, groups):
    return lax.all_to_all(value, AXES, 0, 0, tiled=True, axis_index_groups=groups)


def dot(a, b, dims):
    return lax.dot_general(a, b, (dims, ((), ())), preferred_element_type=jnp.float32)


HBM = pl.BlockSpec(memory_space=pltpu.HBM)
LOCAL = pl.BlockSpec(memory_space=pltpu.VMEM)
EITHER = pl.BlockSpec(memory_space=pl.ANY)


def run(kernel, table, args, outs, scratch, copies, flops, moved, local=(), pinned=(), vmem=SMALL):
    where = {i: LOCAL for i in local} | {i: HBM for i in pinned}
    return pl.pallas_call(
        kernel,
        grid_spec=pltpu.PrefetchScalarGridSpec(
            num_scalar_prefetch=1,
            grid=(),
            in_specs=[where.get(i, EITHER) for i in range(len(args))],
            out_specs=[HBM] * len(outs),
            scratch_shapes=[pltpu.VMEM(shape, dtype) for shape, dtype in scratch]
            + [pltpu.SemaphoreType.DMA((copies,))],
        ),
        out_shape=outs,
        cost_estimate=pl.CostEstimate(flops=flops, bytes_accessed=moved, transcendentals=0),
        compiler_params=pltpu.CompilerParams(vmem_limit_bytes=vmem),
    )(table, *args)


class Copies:
    def __init__(self, sems):
        self.sems, self.used = sems, 0

    def __call__(self, source, target):
        copy = pltpu.make_async_copy(source, target, self.sems.at[self.used])
        self.used += 1
        copy.start()
        return copy


def fetch_pieces(copies, table, phase, own, other, pieces, blocks, basis):
    half, (depth, low_rank) = own.shape[0], pieces[0].shape
    low, started = low_rank // 2, []
    lanes = pl.ds(pl.multiple_of(table[CORE] * low, low), low)
    for j, piece in enumerate(pieces):
        at = pl.ds(j * depth, depth)
        columns = pl.ds(pl.multiple_of(table[PIECES[phase] + j] * depth, depth), depth)
        started += [
            copies(own.at[:, columns], blocks.at[:half, at]),
            copies(other.at[:, columns], blocks.at[half:, at]),
            copies(piece.at[:, lanes], basis.at[at, :]),
        ]
    return started


def wait(copies):
    for copy in copies:
        copy.wait()


def project(table, phase, own, other, pieces, before=None, vmem=SMALL):
    n, half = len(pieces), own.shape[0]
    depth, low = pieces[0].shape[0], pieces[0].shape[1] // 2
    total = jax.ShapeDtypeStruct((2 * half, low), jnp.float32)
    extra = [] if before is None else [before]

    def kernel(table, own, other, *refs):
        pieces, (out, blocks, basis, total, sems) = refs[:n], refs[-5:]
        copies = Copies(sems)
        started = fetch_pieces(copies, table, phase, own, other, pieces, blocks, basis)
        if extra:
            started.append(copies(refs[n], total))
        wait(started)
        ended = []
        for m in range(4):
            rows = pl.ds(m * half // 2, half // 2)
            part = dot(blocks[rows, :], basis[...], ((1,), (0,)))
            total[rows, :] = total[rows, :] + part if extra else part
            ended.append(copies(total.at[rows, :], out.at[rows, :]))
        wait(ended)

    return run(
        kernel,
        table,
        (own, other, *pieces, *extra),
        [total],
        [
            ((2 * half, n * depth), jnp.bfloat16),
            ((n * depth, low), jnp.bfloat16),
            (total.shape, jnp.float32),
        ],
        3 * n + 5,
        4 * half * depth * n * low,
        n * 2**20,
        pinned=(0,),
        vmem=vmem,
    )[0]


def write_tiles(sems, table, call, near, far, projected, dealt, outs):
    def each_out(j, h, act):
        at = TILES[call] + 5 * j + 1 + 2 * h
        for w, out in enumerate(outs):

            @pl.when(table[at] == w)
            def _(out=out):
                target = out.at[table[at + 1]]
                act(pltpu.make_async_copy(dealt.at[j, h], target, sems.at[2 * j + h]))

    for j in range(4):
        cols, half = near.shape[1] // 8, near.shape[0]
        at = table[TILES[call] + 5 * j]
        columns = pl.ds(pl.multiple_of(at * cols, cols), cols)
        total = dot(near[:, columns], projected[:half, :], ((0,), (0,)))
        total += dot(far[:, columns], projected[half:, :], ((0,), (0,)))
        total = total.astype(jnp.bfloat16)
        for h in range(2):
            for z in range(NZ):
                for c in range(2):
                    row = c * 256 + z * 32 + h * 16
                    to = z * 32 + c * 16
                    dealt[j, h, to : to + 16, :] = total[row : row + 16, :]
            each_out(j, h, lambda copy: copy.start())
    for j in range(4):
        for h in range(2):
            each_out(j, h, lambda copy: copy.wait())


def gradient_shapes(near, low):
    half, width = near.shape
    cols = width // 8
    slots = jax.ShapeDtypeStruct((2, cols // 2, low), jnp.bfloat16)
    scratch = [
        ((2 * half, low), jnp.bfloat16),
        ((4, 2, cols // 2, low), jnp.bfloat16),
    ]
    return slots, scratch


def finish(table, own, other, pieces, before, near, far):
    half, width = own.shape
    n, depth, low = len(pieces), pieces[0].shape[0], pieces[0].shape[1] // 2
    slots, scratch = gradient_shapes(near, low)

    def kernel(table, own, other, *refs):
        pieces, (before, near, far, out) = refs[:n], refs[n : n + 4]
        outs, (blocks, basis, projected, dealt, sems) = refs[n + 4 : -5], refs[-5:]
        copies = Copies(sems.at[pl.ds(8, 3 * n + 2)])
        started = fetch_pieces(copies, table, 2, own, other, pieces, blocks, basis)
        wait(started)
        for m in range(4):
            rows = pl.ds(m * half // 2, half // 2)
            part = dot(blocks[rows, :], basis[...], ((1,), (0,)))
            projected[rows, :] = (before[rows, :] + part).astype(projected.dtype)
        kept = copies(projected, out)
        write_tiles(sems, table, 0, near, far, projected, dealt, outs)
        kept.wait()

    return run(
        kernel,
        table,
        (own, other, *pieces, before, near, far),
        [jax.ShapeDtypeStruct((2 * half, low), jnp.bfloat16)] + [slots] * 4,
        [
            ((2 * half, n * depth), jnp.bfloat16),
            ((n * depth, low), jnp.bfloat16),
            *scratch,
        ],
        3 * n + 10,
        2 * half * width * low,
        11 * 2**20,
        local=(n + 2, n + 3, n + 4),
        pinned=(0,),
    )


def gradient(table, near, far, projected):
    half, width = near.shape
    low = projected.shape[1]
    slots, scratch = gradient_shapes(near, low)

    def kernel(table, near, far, source, *refs):
        outs, (projected, dealt, sems) = refs[:4], refs[4:]
        Copies(sems.at[pl.ds(8, 1)])(source, projected).wait()
        write_tiles(sems, table, 1, near, far, projected, dealt, outs)

    return run(
        kernel,
        table,
        (near, far, projected),
        [slots] * 4,
        scratch,
        9,
        2 * half * width * low,
        7 * 2**20,
        local=(0, 1),
    )


def expand(table, mine, rest, update, weight):
    depth, low_rank = mine[0].shape
    cols = weight.shape[1]
    n = len(mine)

    def kernel(table, *refs):
        pieces, (factor, weight, out, new, sems) = refs[: 2 * n], refs[2 * n :]
        copies = Copies(sems)
        ended = []
        for j in range(n):
            for i, side in ((j, table[CORE]), (n + j, 1 - table[CORE])):
                at = pl.multiple_of((2 * table[SHARDS + j] + side) * depth, depth)
                rows = pl.ds(at, depth)
                total = dot(pieces[i][...], factor[...], ((1,), (1,)))
                new[i] = (weight[rows, :].astype(jnp.float32) - rate * total).astype(new.dtype)
                ended.append(copies(new.at[i], out.at[rows, :]))
        wait(ended)

    args = (*mine, *rest, update, weight)
    return run(
        kernel,
        table,
        args,
        [jax.ShapeDtypeStruct(weight.shape, weight.dtype)],
        [((2 * n, depth, cols), jnp.bfloat16)],
        2 * n,
        2 * weight.size * low_rank,
        13 * 2**20,
        local=range(len(args)),
    )[0]


def added(*values):
    return sum(v.astype(jnp.float32) for v in values).astype(jnp.bfloat16)


def tile_rows(core, x, y, call):
    low, rows = y % 2, []
    for j in range(4):
        if core == 0:
            rows.append((j % 2) * 4 + (x + ((2, 0), (1, 3))[call][j // 2]) % 4)
            for h in range(2):
                slot = (h * 2 + j % 2 - y) % 4
                rows += [j // 2 * 2 + slot // 2, slot % 2]
        else:
            side = low if call == 0 else 1 - low
            rows.append(side * 4 + (x + j) % 4)
            for h in range(2):
                which = int((h * 2 + side - y) % 4 != 2 - call)
                rows += [which * 2 + j // 2, j % 2]
    return rows


TURNED = [4 * (j // 4) + (4 - j) % 4 for j in range(8)]
PHASES = ((0, 1, 4), (2, 5, 3, 6), (7,))
CORE, SHARDS, TILES, PIECES = 0, 1, (9, 29), (49, 55, 63)


def device_row(x, y, core):
    shards = [((y + j // 4) % 2) * 4 + (x + (2 * core - 1) * j) % 4 for j in range(8)]
    row = [core] + shards
    for call in range(2):
        row += tile_rows(core, x, y, call)
    for phase in PHASES:
        for j in phase:
            row += [2 * shards[j] + core, 2 * shards[TURNED[j]] + 1 - core]
    return row


def device_table():
    rows = {place(x, y, z, c): device_row(x, y, c) for x, y, z in CHIPS for c in range(2)}
    return np.array([rows[i] for i in range(len(rows))], np.int32)


def body(activations, cotangent, basis, weight, first, second):
    low_rank = basis.shape[1]
    half = low_rank // 2
    owned = first.shape[-1]
    f, d = lax.axis_index("fsdp"), lax.axis_index("dp")
    table = lax.dynamic_index_in_dim(device_table(), d * 16 + f, 0, keepdims=False)

    other_activations, s_x0, y0, x1 = together(
        swap(activations), swap(basis), ring_y(basis), ring_x(basis)
    )
    s_y0, s_x1, y1, x2, x1, y0 = together(
        swap(y0), swap(x1), ring_y(x1), ring_x(x1), x1, y0
    )
    both = (activations, other_activations)
    begun = project(table, 0, *both, [basis, s_x0, x1, s_x1, y0, s_y0], vmem=LARGE)
    s_y1, s_x2, y2, x3, begun, x2, y1, cotangent = together(
        swap(y1), swap(x2), ring_y(x2), ring_x(x2), begun, x2, y1, cotangent
    )
    cotangent, s_x3, s_y2 = together(cotangent, swap(x3), swap(y2))
    other_cotangent = swap(cotangent)
    begun = project(table, 1, *both, [x2, s_x2, y1, s_y1, x3, s_x3, y2, s_y2], begun, SMALL)
    other_cotangent, y3, begun = together(other_cotangent, ring_y(x3), begun)
    s_y3 = swap(y3)
    projected, *opposite_own = finish(
        table, *both, (y3, s_y3), begun, cotangent, other_cotangent
    )
    mine = (basis, x1, x2, x3, y0, y1, y2, y3)
    rest = (s_x0, s_x1, s_x2, s_x3, s_y0, s_y1, s_y2, s_y3)
    rest = tuple(rest[j] for j in TURNED)

    opposite_a, opposite_b, own_a, own_b = opposite_own
    came_a, came_b = along(opposite_a, 1, True), along(opposite_b, -1, True)
    next_a, next_b, last_a, last_b = gradient(table, cotangent, other_cotangent, projected)
    next_b, last_a = along(next_b, 1, True), along(last_a, -1, True)
    next_a = along(added(next_a, came_a), 1, True)
    last_b = along(added(last_b, came_b), -1, True)
    own, following, opposite, previous = [
        added(*(t[i] for t in terms))
        for terms in ((own_a, next_a, last_a), (own_b, next_b, last_b))
        for i in range(2)
    ]
    terms = added(
        own,
        along(opposite, 2, False),
        along(following, 1, False),
        along(previous, -1, False),
    )
    terms = exchange(terms.reshape(16, owned, half), along_zc())
    summed = jnp.sum(terms.reshape(NZ, 2, owned, half).astype(jnp.float32), axis=0)
    summed = summed.transpose(1, 0, 2).reshape(owned, low_rank)

    moment_one = beta_one * first.reshape(low_rank, owned).T + (1.0 - beta_one) * summed
    moment_two = beta_two * second.reshape(low_rank, owned).T + (1.0 - beta_two) * summed * summed
    update = moment_one / corr_one / (jnp.sqrt(moment_two / corr_two) + epsilon)
    update = update.astype(jnp.bfloat16)
    copies = jnp.broadcast_to(update[None], (16, owned, low_rank))
    update = lax.all_to_all(copies, "dp", 0, 0, tiled=True).reshape(16 * owned, low_rank)

    new_weight = expand(table, mine, rest, update, weight)
    return (new_weight, moment_one.T.reshape(first.shape), moment_two.T.reshape(first.shape))


def solution(mesh):
    in_specs = (
        P(("dp", "fsdp"), None),
        P(("dp", "fsdp"), None),
        P("fsdp", None),
        P(None, "fsdp"),
        P(None, "fsdp", "dp", None),
        P(None, "fsdp", "dp", None),
    )
    out_specs = (P(None, "fsdp"), P(None, "fsdp", "dp", None), P(None, "fsdp", "dp", None))
    return jax.shard_map(body, mesh=mesh, in_specs=in_specs, out_specs=out_specs, check_vma=False)
```

```python
import math

import jax
import jax.numpy as jnp
import numpy as np
from jax import lax
from jax.experimental import pallas as pl
from jax.experimental.pallas import tpu as pltpu
from jax.sharding import PartitionSpec as P

beta_one = 0.9
beta_two = 0.999
corr_one = 1.0 - math.exp(1000.0 * math.log(0.9))
corr_two = 1.0 - math.exp(1000.0 * math.log(0.999))
epsilon = 1e-08
rate = 0.5

AXES = ("dp", "fsdp")
NX, NY, NZ = 4, 4, 8
SMALL, LARGE = 16 * 2**20, 56 * 2**20


def place(x, y, z, c):
    return (z * 2 + y // 2) * 16 + ((y % 2) * 4 + x) * 2 + c


CHIPS = [(x, y, z) for z in range(NZ) for y in range(NY) for x in range(NX)]


def route(value, where):
    pairs = []
    for x, y, z in CHIPS:
        for c in range(2):
            tx, ty, tz, tc = where(x, y, z, c)
            pairs.append((place(x, y, z, c), place(tx % NX, ty % NY, tz % NZ, tc)))
    return lax.ppermute(value, AXES, sorted(pairs))


def swap(value):
    return route(value, lambda x, y, z, c: (x, y, z, 1 - c))


def ring_x(value):
    return route(value, lambda x, y, z, c: (x + 1 - 2 * c, y, z, c))


def ring_y(value):
    return route(value, lambda x, y, z, c: (x, y + 1 - 2 * c, z, c))


def along(value, by, first):
    return route(
        value,
        lambda x, y, z, c: (x + by, y, z, c) if (c == 0) == first else (x, y + by, z, c),
    )


def together(*values):
    return lax.optimization_barrier(values)


def along_zc():
    return [
        [place(x, y, z, c) for z in range(NZ) for c in range(2)]
        for y in range(NY)
        for x in range(NX)
    ]


def exchange(value, groups):
    return lax.all_to_all(value, AXES, 0, 0, tiled=True, axis_index_groups=groups)


def dot(a, b, dims):
    return lax.dot_general(a, b, (dims, ((), ())), preferred_element_type=jnp.float32)


HBM = pl.BlockSpec(memory_space=pltpu.HBM)
LOCAL = pl.BlockSpec(memory_space=pltpu.VMEM)
EITHER = pl.BlockSpec(memory_space=pl.ANY)


def run(kernel, table, args, outs, scratch, copies, flops, moved, local=(), pinned=(), vmem=SMALL, here=False):
    where = {i: LOCAL for i in local} | {i: HBM for i in pinned}
    return pl.pallas_call(
        kernel,
        grid_spec=pltpu.PrefetchScalarGridSpec(
            num_scalar_prefetch=1,
            grid=(),
            in_specs=[where.get(i, EITHER) for i in range(len(args))],
            out_specs=[LOCAL if here else HBM] * len(outs),
            scratch_shapes=[pltpu.VMEM(shape, dtype) for shape, dtype in scratch]
            + [pltpu.SemaphoreType.DMA((copies,))],
        ),
        out_shape=outs,
        cost_estimate=pl.CostEstimate(flops=flops, bytes_accessed=moved, transcendentals=0),
        compiler_params=pltpu.CompilerParams(vmem_limit_bytes=vmem),
    )(table, *args)


class Copies:
    def __init__(self, sems):
        self.sems, self.used = sems, 0

    def __call__(self, source, target):
        copy = pltpu.make_async_copy(source, target, self.sems.at[self.used])
        self.used += 1
        copy.start()
        return copy


def fetch_pieces(copies, table, phase, own, other, pieces, blocks, basis=None):
    half, (depth, low_rank) = own.shape[0], pieces[0].shape
    low, started = low_rank // 2, []
    lanes = pl.ds(pl.multiple_of(table[CORE] * low, low), low)
    for j, piece in enumerate(pieces):
        at = pl.ds(j * depth, depth)
        columns = pl.ds(pl.multiple_of(table[PIECES[phase] + j] * depth, depth), depth)
        started += [
            copies(own.at[:, columns], blocks.at[:half, at]),
            copies(other.at[:, columns], blocks.at[half:, at]),
        ]
        if basis is not None:
            started.append(copies(piece.at[:, lanes], basis.at[at, :]))
    return started


def wait(copies):
    for copy in copies:
        copy.wait()


def project(table, phase, own, other, pieces, vmem=SMALL):
    n, half = len(pieces), own.shape[0]
    depth, low = pieces[0].shape[0], pieces[0].shape[1] // 2
    total = jax.ShapeDtypeStruct((2 * half, low), jnp.float32)

    def kernel(table, own, other, *refs):
        pieces, (out, blocks, basis, total, sems) = refs[:n], refs[n:]
        copies = Copies(sems)
        wait(fetch_pieces(copies, table, phase, own, other, pieces, blocks, basis))
        ended = []
        for m in range(4):
            rows = pl.ds(m * half // 2, half // 2)
            total[rows, :] = dot(blocks[rows, :], basis[...], ((1,), (0,)))
            ended.append(copies(total.at[rows, :], out.at[rows, :]))
        wait(ended)

    return run(
        kernel,
        table,
        (own, other, *pieces),
        [total],
        [
            ((2 * half, n * depth), jnp.bfloat16),
            ((n * depth, low), jnp.bfloat16),
            (total.shape, jnp.float32),
        ],
        3 * n + 4,
        4 * half * depth * n * low,
        n * 2**20,
        pinned=(0,),
        vmem=vmem,
    )[0]


def write_tiles(table, call, near, far, projected, outs):
    for j in range(4):
        cols, half = near.shape[1] // 8, near.shape[0]
        at = TILES[call] + 5 * j
        columns = pl.ds(pl.multiple_of(table[at] * cols, cols), cols)
        total = dot(near[:, columns], projected[:half, :], ((0,), (0,)))
        total += dot(far[:, columns], projected[half:, :], ((0,), (0,)))
        total = total.astype(jnp.bfloat16)
        for h in range(2):
            which, slot = table[at + 1 + 2 * h], table[at + 2 + 2 * h]
            for w, out in enumerate(outs):

                @pl.when(which == w)
                def _(out=out, slot=slot, total=total, h=h):
                    for z in range(NZ):
                        for c in range(2):
                            row = c * 256 + z * 32 + h * 16
                            to = z * 32 + c * 16
                            out[slot, to : to + 16, :] = total[row : row + 16, :]


def gradient_shapes(near, low):
    half, width = near.shape
    cols = width // 8
    slots = jax.ShapeDtypeStruct((2, cols // 2, low), jnp.bfloat16)
    return slots


def finish(table, own, other, pieces, parts, near, far):
    half, width = own.shape
    n, depth, low = len(pieces), pieces[0].shape[0], pieces[0].shape[1] // 2
    slots = gradient_shapes(near, low)

    def kernel(table, own, other, *refs):
        pieces, (one, two, near, far, projected) = refs[:n], refs[n : n + 5]
        outs, (blocks, basis, sems) = refs[n + 5 : -3], refs[-3:]
        copies = Copies(sems)
        started = fetch_pieces(copies, table, 2, own, other, pieces, blocks)
        lanes = pl.ds(pl.multiple_of(table[CORE] * low, low), low)
        for j, piece in enumerate(pieces):
            basis[j * depth : (j + 1) * depth, :] = piece[:, lanes]
        wait(started)
        for m in range(4):
            rows = pl.ds(m * half // 2, half // 2)
            part = dot(blocks[rows, :], basis[...], ((1,), (0,)))
            part += one[rows, :] + two[rows, :]
            projected[rows, :] = part.astype(projected.dtype)
        write_tiles(table, 0, near, far, projected, outs)

    return run(
        kernel,
        table,
        (own, other, *pieces, *parts, near, far),
        [jax.ShapeDtypeStruct((2 * half, low), jnp.bfloat16)] + [slots] * 4,
        [
            ((2 * half, n * depth), jnp.bfloat16),
            ((n * depth, low), jnp.bfloat16),
        ],
        2 * n,
        2 * half * width * low,
        11 * 2**20,
        local=range(2, n + 6),
        here=True,
        pinned=(0,),
    )


def gradient(table, near, far, projected):
    half, width = near.shape
    low = projected.shape[1]
    slots = gradient_shapes(near, low)

    def kernel(table, near, far, source, *refs):
        outs = refs[:4]
        write_tiles(table, 1, near, far, source, outs)

    return run(
        kernel,
        table,
        (near, far, projected),
        [slots] * 4,
        [],
        1,
        2 * half * width * low,
        7 * 2**20,
        local=(0, 1, 2),
        here=True,
    )


def assemble(table, mine, rest):
    depth, low_rank = mine[0].shape
    n = len(mine)

    def kernel(table, *refs):
        out, sems = refs[2 * n :]
        copies, started = Copies(sems), []
        for j in range(n):
            for i, side in ((j, table[CORE]), (n + j, 1 - table[CORE])):
                at = pl.multiple_of((2 * table[SHARDS + j] + side) * depth, depth)
                started.append(copies(refs[i], out.at[pl.ds(at, depth), :]))
        wait(started)

    return run(
        kernel,
        table,
        (*mine, *rest),
        [jax.ShapeDtypeStruct((2 * n * depth, low_rank), jnp.bfloat16)],
        [],
        2 * n,
        0,
        16 * 2**20,
        here=True,
    )[0]


def expand(table, rows, update, weight):
    parts = 4
    size, cols = weight.shape[0] // parts, weight.shape[1]

    def kernel(table, rows, update, weight, out, new, sems):
        copies, ended = Copies(sems), []
        for i in range(parts):
            at = pl.ds(i * size, size)
            total = dot(rows[at, :], update[...], ((1,), (1,)))
            new[i] = (weight[at, :].astype(jnp.float32) - rate * total).astype(new.dtype)
            ended.append(copies(new.at[i], out.at[at, :]))
        wait(ended)

    return run(
        kernel,
        table,
        (rows, update, weight),
        [jax.ShapeDtypeStruct(weight.shape, weight.dtype)],
        [((parts, size, cols), jnp.bfloat16)],
        parts,
        2 * weight.size * rows.shape[1],
        13 * 2**20,
        local=range(3),
    )[0]


def added(*values):
    return sum(v.astype(jnp.float32) for v in values).astype(jnp.bfloat16)


def tile_rows(core, x, y, call):
    low, rows = y % 2, []
    for j in range(4):
        if core == 0:
            rows.append((j % 2) * 4 + (x + ((2, 0), (1, 3))[call][j // 2]) % 4)
            for h in range(2):
                slot = (h * 2 + j % 2 - y) % 4
                rows += [j // 2 * 2 + slot // 2, slot % 2]
        else:
            side = low if call == 0 else 1 - low
            rows.append(side * 4 + (x + j) % 4)
            for h in range(2):
                which = int((h * 2 + side - y) % 4 != 2 - call)
                rows += [which * 2 + j // 2, j % 2]
    return rows


TURNED = [4 * (j // 4) + (4 - j) % 4 for j in range(8)]
ORDER = (0, 8, 1, 9, 4, 12, 2, 10, 5, 13, 3, 6, 11, 14, 7, 15)
CORE, SHARDS, TILES, PIECES = 0, 1, (9, 29), (49, 55, 61)


def device_row(x, y, core):
    shards = [((y + j // 4) % 2) * 4 + (x + (2 * core - 1) * j) % 4 for j in range(8)]
    row = [core] + shards
    for call in range(2):
        row += tile_rows(core, x, y, call)
    for j in ORDER:
        if j < 8:
            row.append(2 * shards[j] + core)
        else:
            row.append(2 * shards[TURNED[j - 8]] + 1 - core)
    return row


def device_table():
    rows = {place(x, y, z, c): device_row(x, y, c) for x, y, z in CHIPS for c in range(2)}
    return np.array([rows[i] for i in range(len(rows))], np.int32)


def body(activations, cotangent, basis, weight, first, second):
    low_rank = basis.shape[1]
    half = low_rank // 2
    owned = first.shape[-1]
    f, d = lax.axis_index("fsdp"), lax.axis_index("dp")
    table = lax.dynamic_index_in_dim(device_table(), d * 16 + f, 0, keepdims=False)

    other_activations, s_x0, y0, x1 = together(
        swap(activations), swap(basis), ring_y(basis), ring_x(basis)
    )
    s_y0, s_x1, y1, x2, x1, y0 = together(
        swap(y0), swap(x1), ring_y(x1), ring_x(x1), x1, y0
    )
    both = (activations, other_activations)
    early = project(table, 0, *both, [basis, s_x0, x1, s_x1, y0, s_y0], LARGE)
    s_y1, s_x2, y2, x3, early, x2, y1, cotangent = together(
        swap(y1), swap(x2), ring_y(x2), ring_x(x2), early, x2, y1, cotangent
    )
    late = project(table, 1, *both, [x2, s_x2, y1, s_y1, x3, y2])
    other_cotangent, s_x3, s_y2, y3, late, x3, y2 = together(
        swap(cotangent), swap(x3), swap(y2), ring_y(x3), late, x3, y2
    )
    s_y3 = swap(y3)
    projected, *opposite_own = finish(
        table, *both, (s_x3, s_y2, y3, s_y3), (early, late), cotangent, other_cotangent
    )
    mine = (basis, x1, x2, x3, y0, y1, y2, y3)
    rest = (s_x0, s_x1, s_x2, s_x3, s_y0, s_y1, s_y2, s_y3)
    rest = tuple(rest[j] for j in TURNED)

    opposite_a, opposite_b, own_a, own_b = opposite_own
    came_a, came_b = along(opposite_a, 1, True), along(opposite_b, -1, True)
    next_a, next_b, last_a, last_b = gradient(table, cotangent, other_cotangent, projected)
    next_b, last_a = along(next_b, 1, True), along(last_a, -1, True)
    next_a = along(added(next_a, came_a), 1, True)
    last_b = along(added(last_b, came_b), -1, True)
    own, following, opposite, previous = [
        added(*(t[i] for t in terms))
        for terms in ((own_a, next_a, last_a), (own_b, next_b, last_b))
        for i in range(2)
    ]
    rows = assemble(table, mine, rest)
    rows, own = together(rows, own)
    terms = added(
        own,
        along(opposite, 2, False),
        along(following, 1, False),
        along(previous, -1, False),
    )
    terms = exchange(terms.reshape(16, owned, half), along_zc())
    summed = jnp.sum(terms.reshape(NZ, 2, owned, half).astype(jnp.float32), axis=0)
    summed = summed.transpose(1, 0, 2).reshape(owned, low_rank)

    moment_one = beta_one * first.reshape(low_rank, owned).T + (1.0 - beta_one) * summed
    moment_two = beta_two * second.reshape(low_rank, owned).T + (1.0 - beta_two) * summed * summed
    update = moment_one / corr_one / (jnp.sqrt(moment_two / corr_two) + epsilon)
    update = update.astype(jnp.bfloat16)
    copies = jnp.broadcast_to(update[None], (16, owned, low_rank))
    update = lax.all_to_all(copies, "dp", 0, 0, tiled=True).reshape(16 * owned, low_rank)

    new_weight = expand(table, rows, update, weight)
    return (new_weight, moment_one.T.reshape(first.shape), moment_two.T.reshape(first.shape))


def solution(mesh):
    in_specs = (
        P(("dp", "fsdp"), None),
        P(("dp", "fsdp"), None),
        P("fsdp", None),
        P(None, "fsdp"),
        P(None, "fsdp", "dp", None),
        P(None, "fsdp", "dp", None),
    )
    out_specs = (P(None, "fsdp"), P(None, "fsdp", "dp", None), P(None, "fsdp", "dp", None))
    return jax.shard_map(body, mesh=mesh, in_specs=in_specs, out_specs=out_specs, check_vma=False)
```

```python
import math

import jax
import jax.numpy as jnp
import numpy as np
from jax import lax
from jax.experimental import pallas as pl
from jax.experimental.pallas import tpu as pltpu
from jax.sharding import PartitionSpec as P

beta_one = 0.9
beta_two = 0.999
corr_one = 1.0 - math.exp(1000.0 * math.log(0.9))
corr_two = 1.0 - math.exp(1000.0 * math.log(0.999))
epsilon = 1e-08
rate = 0.5

AXES = ("dp", "fsdp")
NX, NY, NZ = 4, 4, 8
SMALL, LARGE = 16 * 2**20, 56 * 2**20


def place(x, y, z, c):
    return (z * 2 + y // 2) * 16 + ((y % 2) * 4 + x) * 2 + c


CHIPS = [(x, y, z) for z in range(NZ) for y in range(NY) for x in range(NX)]


def route(value, where):
    pairs = []
    for x, y, z in CHIPS:
        for c in range(2):
            tx, ty, tz, tc = where(x, y, z, c)
            pairs.append((place(x, y, z, c), place(tx % NX, ty % NY, tz % NZ, tc)))
    return lax.ppermute(value, AXES, sorted(pairs))


def swap(value):
    return route(value, lambda x, y, z, c: (x, y, z, 1 - c))


def ring_x(value):
    return route(value, lambda x, y, z, c: (x + 1 - 2 * c, y, z, c))


def ring_y(value):
    return route(value, lambda x, y, z, c: (x, y + 1 - 2 * c, z, c))


def along(value, by, first):
    return route(
        value,
        lambda x, y, z, c: (x + by, y, z, c) if (c == 0) == first else (x, y + by, z, c),
    )


def together(*values):
    return lax.optimization_barrier(values)


def along_zc():
    return [
        [place(x, y, z, c) for z in range(NZ) for c in range(2)]
        for y in range(NY)
        for x in range(NX)
    ]


def exchange(value, groups):
    return lax.all_to_all(value, AXES, 0, 0, tiled=True, axis_index_groups=groups)


def dot(a, b, dims):
    return lax.dot_general(a, b, (dims, ((), ())), preferred_element_type=jnp.float32)


HBM = pl.BlockSpec(memory_space=pltpu.HBM)
LOCAL = pl.BlockSpec(memory_space=pltpu.VMEM)
EITHER = pl.BlockSpec(memory_space=pl.ANY)


def run(kernel, table, args, outs, scratch, copies, flops, moved, local=(), pinned=(), vmem=SMALL, here=False):
    where = {i: LOCAL for i in local} | {i: HBM for i in pinned}
    return pl.pallas_call(
        kernel,
        grid_spec=pltpu.PrefetchScalarGridSpec(
            num_scalar_prefetch=1,
            grid=(),
            in_specs=[where.get(i, EITHER) for i in range(len(args))],
            out_specs=[LOCAL if here else HBM] * len(outs),
            scratch_shapes=[pltpu.VMEM(shape, dtype) for shape, dtype in scratch]
            + [pltpu.SemaphoreType.DMA((copies,))],
        ),
        out_shape=outs,
        cost_estimate=pl.CostEstimate(flops=flops, bytes_accessed=moved, transcendentals=0),
        compiler_params=pltpu.CompilerParams(vmem_limit_bytes=vmem),
    )(table, *args)


class Copies:
    def __init__(self, sems):
        self.sems, self.used = sems, 0

    def __call__(self, source, target):
        copy = pltpu.make_async_copy(source, target, self.sems.at[self.used])
        self.used += 1
        copy.start()
        return copy


def fetch_pieces(copies, table, phase, own, other, pieces, blocks, basis=None):
    half, (depth, low_rank) = own.shape[0], pieces[0].shape
    low, started = low_rank // 2, []
    lanes = pl.ds(pl.multiple_of(table[CORE] * low, low), low)
    for j, piece in enumerate(pieces):
        at = pl.ds(j * depth, depth)
        columns = pl.ds(pl.multiple_of(table[PIECES[phase] + j] * depth, depth), depth)
        started += [
            copies(own.at[:, columns], blocks.at[:half, at]),
            copies(other.at[:, columns], blocks.at[half:, at]),
        ]
        if basis is not None:
            started.append(copies(piece.at[:, lanes], basis.at[at, :]))
    return started


def wait(copies):
    for copy in copies:
        copy.wait()


def project(table, phase, own, other, pieces, vmem=SMALL):
    n, half = len(pieces), own.shape[0]
    depth, low = pieces[0].shape[0], pieces[0].shape[1] // 2
    total = jax.ShapeDtypeStruct((2 * half, low), jnp.float32)

    def kernel(table, own, other, *refs):
        pieces, (out, blocks, basis, total, sems) = refs[:n], refs[n:]
        copies = Copies(sems)
        wait(fetch_pieces(copies, table, phase, own, other, pieces, blocks, basis))
        ended = []
        for m in range(4):
            rows = pl.ds(m * half // 2, half // 2)
            total[rows, :] = dot(blocks[rows, :], basis[...], ((1,), (0,)))
            ended.append(copies(total.at[rows, :], out.at[rows, :]))
        wait(ended)

    return run(
        kernel,
        table,
        (own, other, *pieces),
        [total],
        [
            ((2 * half, n * depth), jnp.bfloat16),
            ((n * depth, low), jnp.bfloat16),
            (total.shape, jnp.float32),
        ],
        3 * n + 4,
        4 * half * depth * n * low,
        n * 2**20,
        pinned=(0,),
        vmem=vmem,
    )[0]


def write_tiles(table, call, near, far, projected, outs):
    for j in range(4):
        cols, half = near.shape[1] // 8, near.shape[0]
        at = TILES[call] + 5 * j
        columns = pl.ds(pl.multiple_of(table[at] * cols, cols), cols)
        total = dot(near[:, columns], projected[:half, :], ((0,), (0,)))
        total += dot(far[:, columns], projected[half:, :], ((0,), (0,)))
        total = total.astype(jnp.bfloat16)
        for h in range(2):
            which, slot = table[at + 1 + 2 * h], table[at + 2 + 2 * h]
            for w, out in enumerate(outs):

                @pl.when(which == w)
                def _(out=out, slot=slot, total=total, h=h):
                    for z in range(NZ):
                        for c in range(2):
                            row = c * 256 + z * 32 + h * 16
                            to = z * 32 + c * 16
                            out[slot, to : to + 16, :] = total[row : row + 16, :]


def gradient_shapes(near, low):
    half, width = near.shape
    cols = width // 8
    slots = jax.ShapeDtypeStruct((2, cols // 2, low), jnp.bfloat16)
    return slots


def finish(table, own, other, pieces, parts, near, far):
    half, width = own.shape
    n, depth, low = len(pieces), pieces[0].shape[0], pieces[0].shape[1] // 2
    slots = gradient_shapes(near, low)

    def kernel(table, own, other, *refs):
        pieces, (one, two, near, far, projected) = refs[:n], refs[n : n + 5]
        outs, (blocks, basis, sems) = refs[n + 5 : -3], refs[-3:]
        copies = Copies(sems)
        started = fetch_pieces(copies, table, 2, own, other, pieces, blocks)
        lanes = pl.ds(pl.multiple_of(table[CORE] * low, low), low)
        for j, piece in enumerate(pieces):
            basis[j * depth : (j + 1) * depth, :] = piece[:, lanes]
        wait(started)
        for m in range(4):
            rows = pl.ds(m * half // 2, half // 2)
            part = dot(blocks[rows, :], basis[...], ((1,), (0,)))
            part += one[rows, :] + two[rows, :]
            projected[rows, :] = part.astype(projected.dtype)
        write_tiles(table, 0, near, far, projected, outs)

    return run(
        kernel,
        table,
        (own, other, *pieces, *parts, near, far),
        [jax.ShapeDtypeStruct((2 * half, low), jnp.bfloat16)] + [slots] * 4,
        [
            ((2 * half, n * depth), jnp.bfloat16),
            ((n * depth, low), jnp.bfloat16),
        ],
        2 * n,
        2 * half * width * low,
        11 * 2**20,
        local=range(2, n + 6),
        here=True,
        pinned=(0,),
    )


def gradient(table, near, far, projected):
    half, width = near.shape
    low = projected.shape[1]
    slots = gradient_shapes(near, low)

    def kernel(table, near, far, source, *refs):
        outs = refs[:4]
        write_tiles(table, 1, near, far, source, outs)

    return run(
        kernel,
        table,
        (near, far, projected),
        [slots] * 4,
        [],
        1,
        2 * half * width * low,
        7 * 2**20,
        local=(0, 1, 2),
        here=True,
    )


def assemble(table, mine, rest):
    depth, low_rank = mine[0].shape
    n = len(mine)

    def kernel(table, *refs):
        out, sems = refs[2 * n :]
        copies, started = Copies(sems), []
        for j in range(n):
            for i, side in ((j, table[CORE]), (n + j, 1 - table[CORE])):
                at = pl.multiple_of((2 * table[SHARDS + j] + side) * depth, depth)
                started.append(copies(refs[i], out.at[pl.ds(at, depth), :]))
        wait(started)

    return run(
        kernel,
        table,
        (*mine, *rest),
        [jax.ShapeDtypeStruct((2 * n * depth, low_rank), jnp.bfloat16)],
        [],
        2 * n,
        0,
        16 * 2**20,
        here=True,
    )[0]


def expand(table, rows, update, weight):
    parts = 4
    size, cols = weight.shape[0] // parts, weight.shape[1]

    def kernel(table, rows, update, weight, out, new, sems):
        copies, ended = Copies(sems), []
        for i in range(parts):
            at = pl.ds(i * size, size)
            total = dot(rows[at, :], update[...], ((1,), (1,)))
            new[i] = (weight[at, :].astype(jnp.float32) - rate * total).astype(new.dtype)
            ended.append(copies(new.at[i], out.at[at, :]))
        wait(ended)

    return run(
        kernel,
        table,
        (rows, update, weight),
        [jax.ShapeDtypeStruct(weight.shape, weight.dtype)],
        [((parts, size, cols), jnp.bfloat16)],
        parts,
        2 * weight.size * rows.shape[1],
        13 * 2**20,
        local=range(3),
    )[0]


def added(*values):
    return sum(v.astype(jnp.float32) for v in values).astype(jnp.bfloat16)


def tile_rows(core, x, y, call):
    low, rows = y % 2, []
    for j in range(4):
        if core == 0:
            rows.append((j % 2) * 4 + (x + ((2, 0), (1, 3))[call][j // 2]) % 4)
            for h in range(2):
                slot = (h * 2 + j % 2 - y) % 4
                rows += [j // 2 * 2 + slot // 2, slot % 2]
        else:
            side = low if call == 0 else 1 - low
            rows.append(side * 4 + (x + j) % 4)
            for h in range(2):
                which = int((h * 2 + side - y) % 4 != 2 - call)
                rows += [which * 2 + j // 2, j % 2]
    return rows


TURNED = [4 * (j // 4) + (4 - j) % 4 for j in range(8)]
ORDER = (0, 8, 1, 9, 4, 12, 2, 10, 5, 13, 3, 6, 11, 14, 7, 15)
CORE, SHARDS, TILES, PIECES = 0, 1, (9, 29), (49, 55, 61)


def device_row(x, y, core):
    shards = [((y + j // 4) % 2) * 4 + (x + (2 * core - 1) * j) % 4 for j in range(8)]
    row = [core] + shards
    for call in range(2):
        row += tile_rows(core, x, y, call)
    for j in ORDER:
        if j < 8:
            row.append(2 * shards[j] + core)
        else:
            row.append(2 * shards[TURNED[j - 8]] + 1 - core)
    return row


def device_table():
    rows = {place(x, y, z, c): device_row(x, y, c) for x, y, z in CHIPS for c in range(2)}
    return np.array([rows[i] for i in range(len(rows))], np.int32)


def body(activations, cotangent, basis, weight, first, second):
    low_rank = basis.shape[1]
    half = low_rank // 2
    owned = first.shape[-1]
    f, d = lax.axis_index("fsdp"), lax.axis_index("dp")
    table = lax.dynamic_index_in_dim(device_table(), d * 16 + f, 0, keepdims=False)

    other_activations, s_x0, y0, x1 = together(
        swap(activations), swap(basis), ring_y(basis), ring_x(basis)
    )
    s_y0, s_x1, y1, x2, x1, y0 = together(
        swap(y0), swap(x1), ring_y(x1), ring_x(x1), x1, y0
    )
    both = (activations, other_activations)
    early = project(table, 0, *both, [basis, s_x0, x1, s_x1, y0, s_y0], LARGE)
    s_y1, s_x2, y2, x3, early, x2, y1, cotangent = together(
        swap(y1), swap(x2), ring_y(x2), ring_x(x2), early, x2, y1, cotangent
    )
    late = project(table, 1, *both, [x2, s_x2, y1, s_y1, x3, y2])
    top = x3.shape[0] // 2
    other_cotangent, s_x3, s_y2, y3_top, y3_bottom, late, x3, y2 = together(
        swap(cotangent), swap(x3), swap(y2), ring_y(x3[:top]), ring_x(y2[top:]), late, x3, y2
    )
    y3 = jnp.concatenate([y3_top, y3_bottom], axis=0)
    s_y3 = swap(y3)
    projected, *opposite_own = finish(
        table, *both, (s_x3, s_y2, y3, s_y3), (early, late), cotangent, other_cotangent
    )
    mine = (basis, x1, x2, x3, y0, y1, y2, y3)
    rest = (s_x0, s_x1, s_x2, s_x3, s_y0, s_y1, s_y2, s_y3)
    rest = tuple(rest[j] for j in TURNED)

    opposite_a, opposite_b, own_a, own_b = opposite_own
    came_a, came_b = along(opposite_a, 1, True), along(opposite_b, -1, True)
    next_a, next_b, last_a, last_b = gradient(table, cotangent, other_cotangent, projected)
    next_b, last_a = along(next_b, 1, True), along(last_a, -1, True)
    next_a = along(added(next_a, came_a), 1, True)
    last_b = along(added(last_b, came_b), -1, True)
    own, following, opposite, previous = [
        added(*(t[i] for t in terms))
        for terms in ((own_a, next_a, last_a), (own_b, next_b, last_b))
        for i in range(2)
    ]
    rows = assemble(table, mine, rest)
    rows, own = together(rows, own)
    terms = added(
        own,
        along(opposite, 2, False),
        along(following, 1, False),
        along(previous, -1, False),
    )
    terms = exchange(terms.reshape(16, owned, half), along_zc())
    summed = jnp.sum(terms.reshape(NZ, 2, owned, half).astype(jnp.float32), axis=0)
    summed = summed.transpose(1, 0, 2).reshape(owned, low_rank)

    moment_one = beta_one * first.reshape(low_rank, owned).T + (1.0 - beta_one) * summed
    moment_two = beta_two * second.reshape(low_rank, owned).T + (1.0 - beta_two) * summed * summed
    update = moment_one / corr_one / (jnp.sqrt(moment_two / corr_two) + epsilon)
    update = update.astype(jnp.bfloat16)
    copies = jnp.broadcast_to(update[None], (16, owned, low_rank))
    update = lax.all_to_all(copies, "dp", 0, 0, tiled=True).reshape(16 * owned, low_rank)

    new_weight = expand(table, rows, update, weight)
    return (new_weight, moment_one.T.reshape(first.shape), moment_two.T.reshape(first.shape))


def solution(mesh):
    in_specs = (
        P(("dp", "fsdp"), None),
        P(("dp", "fsdp"), None),
        P("fsdp", None),
        P(None, "fsdp"),
        P(None, "fsdp", "dp", None),
        P(None, "fsdp", "dp", None),
    )
    out_specs = (P(None, "fsdp"), P(None, "fsdp", "dp", None), P(None, "fsdp", "dp", None))
    return jax.shard_map(body, mesh=mesh, in_specs=in_specs, out_specs=out_specs, check_vma=False)
```
